512 devices in a mesh: sta: 64 (over x, y, core), day: 8 (over z).
Axes of the slice: x: 4, y: 8, z: 8, core: 2. Of those that a mesh axis runs over, the one named last changes fastest.
Arguments:
- spectra: bfloat16 [8, 4096, 512], P('day', 'sta'), may hold values from -6 to 6
- picks: int32 [64, 64, 8], P('sta'), may hold values from 0 to 63
- pair_own: int32 [65536], P('sta'), may hold values from 0 to 63
- pair_far: int32 [65536], P('sta'), may hold values from 0 to 511
- pair_mask: int32 [65536], P('sta'), may hold values 0 or 1
Outputs:
- stacks: float32 [65536, 1024], P(('sta', 'day'))
The draws below stay inside these ranges and needn't reach their ends.
All inputs are finite; a program needn't handle non-finite values. No bound on the sum of `pair_mask` on one device may be relied on, other than what follows from the above.
Results may differ from the reference program's by a relative error of at most 0.0003.
Values may be sent and summed in bfloat16 or wider, within the bound.
No kernel may reach another device: no remote copies, remote signals or barrier semaphores. Data moves between devices by JAX's collectives and lax.ppermute only.
A program may use at most 64 MiB of HBM per device.

```python
import jax
import jax.numpy as jnp
from jax import lax

STA_DEV = 64
SLOTS = 8
PAIRS = 1024
NF = 256
LAGS = 1024
BASE_BIN = 40
DAYS = 8
STATIONS = 4096
PAIRS_ALL = 65536
N_STA = 64


def with_ends(values, own_key, least, largest):
    place = [jax.random.randint(jax.random.fold_in(own_key, axis), (), 0, length) for axis, length in enumerate(values.shape)]
    main_axis = values.shape.index(max(values.shape))
    beside = place[:main_axis] + [(place[main_axis] + 1) % values.shape[main_axis]] + place[main_axis + 1:]
    return values.at[tuple(place)].set(least).at[tuple(beside)].set(largest)


def levels(stream_key, shape, shards, smallest, top_value):
    def one(position, parts):
        steps = jax.random.uniform(jax.random.fold_in(jax.random.fold_in(stream_key, 6), position), (parts,), jnp.float32, smallest / len(shards), top_value / len(shards))
        return jnp.repeat(jnp.exp(steps), shape[position] // parts).reshape((-1,) + (1,) * (len(shape) - position - 1))

    gain = one(*shards[0])
    for cut in shards[1:]:
        gain = gain * one(*cut)
    return gain


def normal_values(key, dims, spread, bound, cuts=(), held_as=jnp.bfloat16):
    level = levels(key, dims, cuts, -0.22, 0.18) if cuts else 1.0
    result = jax.random.normal(key, dims, jnp.float32) * spread * level
    return jnp.minimum(jnp.maximum(result, -bound), bound).astype(held_as)


def setup_inputs(seed: int = 0) -> dict:
    keys = jax.random.split(jax.random.key(seed), 6)
    spectra = normal_values(keys[0], (DAYS, STATIONS, 2 * NF), 1.0, 6.0, ((0, 8), (1, 64)))
    picks = with_ends(jax.random.randint(keys[1], (N_STA, N_STA, SLOTS), 0, STA_DEV), jax.random.fold_in(keys[1], 1), 0, STA_DEV - 1).astype(jnp.int32)
    pair_own = with_ends(jax.random.randint(keys[2], (PAIRS_ALL,), 0, STA_DEV), jax.random.fold_in(keys[2], 1), 0, STA_DEV - 1).astype(jnp.int32)
    pair_far = with_ends(jax.random.randint(keys[3], (PAIRS_ALL,), 0, N_STA * SLOTS), jax.random.fold_in(keys[3], 1), 0, (N_STA * SLOTS) - 1).astype(jnp.int32)
    pair_mask = with_ends((jax.random.randint(keys[4], (PAIRS_ALL,), 0, 3) < 2).astype(jnp.int32), jax.random.fold_in(keys[4], 1), 0, 1)
    return dict(spectra=spectra, picks=picks, pair_own=pair_own, pair_far=pair_far, pair_mask=pair_mask)


def lag_table(bins, lags, base):
    k = jnp.arange(bins).astype(jnp.int32)[:, None] + base
    m = jnp.arange(lags).astype(jnp.int32)[None, :] - lags // 2
    q = k * m % lags
    angle = 2.0 * jnp.pi / lags * q.astype(jnp.float32)
    return jnp.concatenate([jnp.cos(angle), -jnp.sin(angle)], axis=0)

def reference(spectra, picks, pair_own, pair_far, pair_mask):
    owner = (jnp.arange(PAIRS_ALL) // PAIRS).astype(jnp.int32)
    source = (pair_far // SLOTS).astype(jnp.int32)
    slot_index = (pair_far % SLOTS).astype(jnp.int32)
    second = source * STA_DEV + picks[source, owner, slot_index]
    first = owner * STA_DEV + pair_own
    weight = pair_mask.astype(jnp.float32)[:, None]

    def add_day(total, day_spec):
        near = day_spec[first].astype(jnp.float32)
        far_part = day_spec[second].astype(jnp.float32)
        near_re, near_im = (near[:, :NF], near[:, NF:])
        far_re, far_im = (far_part[:, :NF], far_part[:, NF:])
        real_part = near_re * far_re + near_im * far_im
        imag_part = near_im * far_re - near_re * far_im
        return (total + weight * jnp.concatenate([real_part, imag_part], axis=1), None)
    summed, _ = lax.scan(add_day, jnp.zeros((PAIRS_ALL, 2 * NF), jnp.float32), spectra)
    table = lag_table(NF, LAGS, BASE_BIN)
    scale = 1.0 / jnp.sqrt(jnp.float32(2 * NF * DAYS))
    return jnp.dot(summed, table, precision=lax.Precision.HIGHEST, preferred_element_type=jnp.float32) * scale
```

```python
import jax
import jax.numpy as jnp
import numpy as np
from jax import lax
from jax.experimental import pallas as pl
from jax.experimental.pallas import tpu as pltpu
from jax.sharding import PartitionSpec as P

SLOTS = 8
LAGS = 1024
BASE = 40
BF16 = jnp.bfloat16
F32 = jnp.float32
VMEM = pl.BlockSpec(memory_space=pltpu.VMEM)


def lag_table(bins, n_day, scale):
    k = np.arange(bins)[:, None] + BASE
    m = np.arange(LAGS)[None, :] - LAGS // 2
    angle = 2.0 * np.pi / LAGS * (k * m % LAGS)
    part = bins // n_day
    both = np.stack([np.cos(angle), -np.sin(angle)]) * scale
    both = both.reshape(2, n_day, part, LAGS).transpose(1, 0, 2, 3).reshape(2 * bins, LAGS).astype(np.float32)
    high = both.astype(jnp.bfloat16)
    low = (both - high.astype(np.float32)).astype(jnp.bfloat16)
    return high, low


def turn_kernel(x_ref, out_ref):
    n_day, part, _ = out_ref.shape
    bins = n_day * part
    x = x_ref[0].astype(F32)
    y = jnp.concatenate([x[:, :bins], x[:, bins:]], axis=0)
    out_ref[...] = y.T.astype(BF16).reshape(out_ref.shape)


def pick_kernel(picks_ref, mine_ref, out_ref):
    slots, owners = picks_ref.shape
    n_day, part, twice = mine_ref.shape
    rows = n_day * part
    mine = mine_ref[...].reshape(rows, twice)
    picks = picks_ref[...]
    lane = lax.broadcasted_iota(jnp.int32, (slots, twice), 1)
    for half in range(2):
        hot = jnp.concatenate(
            [(lane == picks[:, o : o + 1] + half * (twice // 2)).astype(F32) for o in range(owners)], axis=0
        ).astype(BF16)
        got = lax.dot_general(hot, mine, (((1,), (1,)), ((), ())), preferred_element_type=F32)
        out_ref[:, :, half * rows : (half + 1) * rows] = got.astype(BF16).reshape(owners, slots, rows)


def cross_kernel(own_ref, far_ref, mask_ref, mine_ref, got_ref, out_ref, turned):
    n_day, part, twice = mine_ref.shape
    rows = n_day * part
    slots = got_ref.shape[0]
    blocks, lanes = own_ref.shape
    mine = mine_ref[...].reshape(rows, twice)
    turned[...] = got_ref[...].astype(F32).T.astype(BF16)
    near_row = lax.broadcasted_iota(jnp.int32, (twice, lanes), 0)
    far_row = lax.broadcasted_iota(jnp.int32, (slots, lanes), 0)
    for j in range(blocks):
        own = jnp.where(mask_ref[j : j + 1, :] > 0, own_ref[j : j + 1, :], 2 * twice)
        far = far_ref[j : j + 1, :]
        hot_re = (near_row == own).astype(F32).astype(BF16)
        hot_im = (near_row == own + twice // 2).astype(F32).astype(BF16)
        hot_far = (far_row == far).astype(F32).astype(BF16)
        near_re = jnp.dot(mine, hot_re, preferred_element_type=F32)
        near_im = jnp.dot(mine, hot_im, preferred_element_type=F32)
        both = jnp.dot(turned[...], hot_far, preferred_element_type=F32)
        far_re, far_im = both[:rows], both[rows:]
        real = near_re * far_re + near_im * far_im
        imag = near_im * far_re - near_re * far_im
        out_ref[j, :part, :] = jnp.sum(real.reshape(n_day, part, lanes), axis=0)
        out_ref[j, part:, :] = jnp.sum(imag.reshape(n_day, part, lanes), axis=0)


def stack_kernel(summed_ref, high_ref, low_ref, out_ref):
    turned = summed_ref[...].T
    high = turned.astype(BF16)
    low = (turned - high.astype(F32)).astype(BF16)
    out = jnp.dot(high, high_ref[...], preferred_element_type=F32)
    out += jnp.dot(low, high_ref[...], preferred_element_type=F32)
    out += jnp.dot(high, low_ref[...], preferred_element_type=F32)
    out_ref[...] = out


def call(kernel, shape, dtype, n_in, scratch=()):
    return pl.pallas_call(
        kernel,
        out_shape=jax.ShapeDtypeStruct(shape, dtype),
        in_specs=[VMEM] * n_in,
        out_specs=VMEM,
        scratch_shapes=list(scratch),
        compiler_params=pltpu.CompilerParams(vmem_limit_bytes=48 * 1024 * 1024),
    )


def local(spectra, picks, pair_own, pair_far, pair_mask):
    n_sta = lax.axis_size("sta")
    n_day = lax.axis_size("day")
    _, stations, width = spectra.shape
    bins = width // 2
    part = bins // n_day
    pairs = pair_own.shape[0]
    mine_pairs = pairs // n_day

    by_bin = call(turn_kernel, (n_day, part, 2 * stations), BF16, 1)(spectra)
    mine = lax.all_to_all(by_bin, "day", split_axis=0, concat_axis=0, tiled=True)
    chosen = call(pick_kernel, (n_sta, SLOTS, width), BF16, 2)(picks[0].T, mine)
    got = lax.all_to_all(chosen, "sta", split_axis=0, concat_axis=0, tiled=True).reshape(n_sta * SLOTS, width)
    by_block = [a.reshape(n_day, mine_pairs) for a in (pair_own, pair_far, pair_mask)]
    cross = call(
        cross_kernel, (n_day, 2 * part, mine_pairs), F32, 5, [pltpu.VMEM((width, n_sta * SLOTS), BF16)]
    )(*by_block, mine, got)
    summed = lax.all_to_all(cross, "day", split_axis=0, concat_axis=0, tiled=True).reshape(width, mine_pairs)
    scale = 1.0 / np.sqrt(width * n_day)
    high, low = lag_table(bins, n_day, scale)
    return call(stack_kernel, (mine_pairs, LAGS), F32, 3)(summed, jnp.asarray(high), jnp.asarray(low))


def solution(mesh):
    in_specs = (P("day", "sta", None), P("sta", None, None), P("sta"), P("sta"), P("sta"))
    out_specs = P(("sta", "day"), None)
    return jax.shard_map(local, mesh=mesh, in_specs=in_specs, out_specs=out_specs, check_vma=False)
```

```python
import jax
import jax.numpy as jnp
import numpy as np
from jax import lax
from jax.experimental import pallas as pl
from jax.experimental.pallas import tpu as pltpu
from jax.sharding import PartitionSpec as P

SLOTS = 8
LAGS = 1024
BASE = 40
BF16 = jnp.bfloat16
F32 = jnp.float32
VMEM = pl.BlockSpec(memory_space=pltpu.VMEM)
HBM = pl.BlockSpec(memory_space=pltpu.HBM)


def lag_table(bins, n_day, scale):
    k = np.arange(bins)[:, None] + BASE
    m = np.arange(LAGS)[None, :] - LAGS // 2
    angle = 2.0 * np.pi / LAGS * (k * m % LAGS)
    part = bins // n_day
    both = np.stack([np.cos(angle), -np.sin(angle)]) * scale
    both = both.reshape(2, n_day, part, LAGS).transpose(1, 0, 2, 3).reshape(2 * bins, LAGS).astype(np.float32)
    high = both.astype(jnp.bfloat16)
    low = (both - high.astype(np.float32)).astype(jnp.bfloat16)
    return high, low


def turn_kernel(x_ref, out_ref):
    n_day, part, _ = out_ref.shape
    bins = n_day * part
    x = x_ref[0].astype(F32)
    y = jnp.concatenate([x[:, :bins], x[:, bins:]], axis=0)
    out_ref[...] = y.T.astype(BF16).reshape(out_ref.shape)


def pick_kernel(picks_ref, mine_ref, out_ref):
    slots, owners = picks_ref.shape
    n_day, part, twice = mine_ref.shape
    rows = n_day * part
    mine = mine_ref[...].reshape(rows, twice)
    picks = picks_ref[...]
    lane = lax.broadcasted_iota(jnp.int32, (slots, twice), 1)
    for half in range(2):
        hot = jnp.concatenate(
            [(lane == picks[:, o : o + 1] + half * (twice // 2)).astype(F32) for o in range(owners)], axis=0
        ).astype(BF16)
        got = lax.dot_general(hot, mine, (((1,), (1,)), ((), ())), preferred_element_type=F32)
        out_ref[:, :, half * rows : (half + 1) * rows] = got.astype(BF16).reshape(owners, slots, rows)


def cross_kernel(own_ref, far_ref, mask_ref, mine_ref, got_ref, out_ref, turned):
    n_day, part, twice = mine_ref.shape
    rows = n_day * part
    blocks, lanes = own_ref.shape
    mine = mine_ref[...].reshape(rows, twice)
    turned[...] = got_ref[...].T
    near_row = lax.broadcasted_iota(jnp.int32, (twice, 2 * lanes), 0)
    far_row = lax.broadcasted_iota(jnp.int32, (got_ref.shape[0], 2 * lanes), 0)
    for j in range(0, blocks, 2):
        own = jnp.where(mask_ref[j : j + 2, :] > 0, own_ref[j : j + 2, :], 2 * twice)
        own = jnp.concatenate([own[:1], own[1:]], axis=1)
        far = jnp.concatenate([far_ref[j : j + 1, :], far_ref[j + 1 : j + 2, :]], axis=1)
        hot_far = (far_row == far).astype(F32).astype(BF16)
        hot_re = (near_row == own).astype(F32).astype(BF16)
        hot_im = (near_row == own + twice // 2).astype(F32).astype(BF16)
        near_re = jnp.dot(mine, hot_re, preferred_element_type=F32)
        near_im = jnp.dot(mine, hot_im, preferred_element_type=F32)
        both = jnp.dot(turned[...], hot_far, preferred_element_type=F32)
        far_re, far_im = both[:rows], both[rows:]
        real = jnp.sum((near_re * far_re + near_im * far_im).reshape(n_day, part, 2 * lanes), axis=0)
        imag = jnp.sum((near_im * far_re - near_re * far_im).reshape(n_day, part, 2 * lanes), axis=0)
        for i in range(2):
            out_ref[j + i, :part, :] = real[:, i * lanes : (i + 1) * lanes]
            out_ref[j + i, part:, :] = imag[:, i * lanes : (i + 1) * lanes]


def stack_kernel(summed_ref, high_ref, low_ref, out_hbm, stage, sems):
    rows, lags = stage.shape
    turned = summed_ref[...].T
    high = turned.astype(BF16)
    low = (turned - high.astype(F32)).astype(BF16)
    both = jnp.concatenate([high, low], axis=0)
    step = lags // 2
    copies = []
    for j in range(2):
        at = slice(j * step, (j + 1) * step)
        out = jnp.dot(both, high_ref[:, at], preferred_element_type=F32)
        stage[:, at] = out[:rows] + out[rows:] + jnp.dot(high, low_ref[:, at], preferred_element_type=F32)
        copies.append(pltpu.make_async_copy(stage.at[:, at], out_hbm.at[:, at], sems.at[j]))
        copies[j].start()
    for copy in copies:
        copy.wait()


def call(kernel, out_shape, in_specs, out_specs, scratch=()):
    return pl.pallas_call(
        kernel,
        out_shape=out_shape,
        in_specs=in_specs,
        out_specs=out_specs,
        scratch_shapes=list(scratch),
        compiler_params=pltpu.CompilerParams(vmem_limit_bytes=48 * 1024 * 1024),
    )


def local(spectra, picks, pair_own, pair_far, pair_mask):
    n_sta = lax.axis_size("sta")
    n_day = lax.axis_size("day")
    _, stations, width = spectra.shape
    bins = width // 2
    part = bins // n_day
    pairs = pair_own.shape[0]
    mine_pairs = pairs // n_day
    slots = n_sta * SLOTS
    shape = jax.ShapeDtypeStruct
    dma = pltpu.SemaphoreType.DMA
    own, far, mask = [a.reshape(n_day, mine_pairs) for a in (pair_own, pair_far, pair_mask)]

    by_bin = call(turn_kernel, shape((n_day, part, 2 * stations), BF16), [VMEM], VMEM)(spectra)
    mine = lax.all_to_all(by_bin, "day", split_axis=0, concat_axis=0, tiled=True)
    chosen = call(pick_kernel, shape((n_sta, SLOTS, width), BF16), [VMEM] * 2, VMEM)(picks[0].T, mine)
    got = lax.all_to_all(chosen, "sta", split_axis=0, concat_axis=0, tiled=True).reshape(slots, width)
    cross = call(
        cross_kernel,
        shape((n_day, 2 * part, mine_pairs), F32),
        [VMEM] * 5,
        VMEM,
        [pltpu.VMEM((width, slots), BF16)],
    )(own, far, mask, mine, got)
    summed = lax.all_to_all(cross, "day", split_axis=0, concat_axis=0, tiled=True).reshape(width, mine_pairs)
    high, low = lag_table(bins, n_day, 1.0 / np.sqrt(width * n_day))
    return call(
        stack_kernel,
        shape((mine_pairs, LAGS), F32),
        [VMEM] * 3,
        HBM,
        [pltpu.VMEM((mine_pairs, LAGS), F32), dma((2,))],
    )(summed, jnp.asarray(high), jnp.asarray(low))


def solution(mesh):
    in_specs = (P("day", "sta", None), P("sta", None, None), P("sta"), P("sta"), P("sta"))
    out_specs = P(("sta", "day"), None)
    return jax.shard_map(local, mesh=mesh, in_specs=in_specs, out_specs=out_specs, check_vma=False)
```

```python
import jax
import jax.numpy as jnp
import numpy as np
from jax import lax
from jax.experimental import pallas as pl
from jax.experimental.pallas import tpu as pltpu
from jax.sharding import PartitionSpec as P

SLOTS = 8
LAGS = 1024
BASE = 40
BF16 = jnp.bfloat16
F32 = jnp.float32
VMEM = pl.BlockSpec(memory_space=pltpu.VMEM)
HBM = pl.BlockSpec(memory_space=pltpu.HBM)


def lag_table(bins, n_day, scale):
    k = np.arange(bins)[:, None] + BASE
    m = np.arange(LAGS)[None, :] - LAGS // 2
    angle = 2.0 * np.pi / LAGS * (k * m % LAGS)
    part = bins // n_day
    both = np.stack([np.cos(angle), -np.sin(angle)]) * scale
    both = both.reshape(2, n_day, part, LAGS).transpose(1, 0, 2, 3).reshape(2 * bins, LAGS).astype(np.float32)
    high = both.astype(jnp.bfloat16)
    low = (both - high.astype(np.float32)).astype(jnp.bfloat16)
    return high, low


def turn_kernel(x_ref, out_ref):
    n_day, part, _ = out_ref.shape
    bins = n_day * part
    x = x_ref[0].astype(F32)
    y = jnp.concatenate([x[:, :bins], x[:, bins:]], axis=0)
    out_ref[...] = y.T.astype(BF16).reshape(out_ref.shape)


def pick_kernel(picks_ref, mine_ref, out_ref):
    slots, owners = picks_ref.shape
    n_day, part, twice = mine_ref.shape
    stations = twice // 2
    turned = mine_ref[...].reshape(n_day * part, twice).T
    source = jnp.concatenate([turned[:stations], turned[stations:]], axis=1)
    picks = picks_ref[...]
    lane = lax.broadcasted_iota(jnp.int32, (slots, stations), 1)
    hot = jnp.concatenate([(lane == picks[:, o : o + 1]).astype(F32) for o in range(owners)], axis=0).astype(BF16)
    got = jnp.dot(hot, source, preferred_element_type=F32)
    out_ref[...] = got.astype(BF16).reshape(out_ref.shape)


def cross_kernel(own_ref, far_ref, mask_ref, mine_ref, got_ref, out_ref, turned):
    n_day, part, twice = mine_ref.shape
    rows = n_day * part
    blocks, lanes = own_ref.shape
    mine = mine_ref[...].reshape(rows, twice)
    turned[...] = got_ref[...].T
    near_row = lax.broadcasted_iota(jnp.int32, (twice, 2 * lanes), 0)
    far_row = lax.broadcasted_iota(jnp.int32, (got_ref.shape[0], 2 * lanes), 0)
    for j in range(0, blocks, 2):
        own = jnp.where(mask_ref[j : j + 2, :] > 0, own_ref[j : j + 2, :], 2 * twice)
        own = jnp.concatenate([own[:1], own[1:]], axis=1)
        far = jnp.concatenate([far_ref[j : j + 1, :], far_ref[j + 1 : j + 2, :]], axis=1)
        hot_far = (far_row == far).astype(F32).astype(BF16)
        both = jnp.dot(turned[...], hot_far, preferred_element_type=F32)
        hot_re = (near_row == own).astype(F32).astype(BF16)
        hot_im = (near_row == own + twice // 2).astype(F32).astype(BF16)
        near_re = jnp.dot(mine, hot_re, preferred_element_type=F32)
        near_im = jnp.dot(mine, hot_im, preferred_element_type=F32)
        far_re, far_im = both[:rows], both[rows:]
        real = jnp.sum((near_re * far_re + near_im * far_im).reshape(n_day, part, 2 * lanes), axis=0)
        imag = jnp.sum((near_im * far_re - near_re * far_im).reshape(n_day, part, 2 * lanes), axis=0)
        for i in range(2):
            out_ref[j + i, :part, :] = real[:, i * lanes : (i + 1) * lanes]
            out_ref[j + i, part:, :] = imag[:, i * lanes : (i + 1) * lanes]


def stack_kernel(summed_ref, high_ref, low_ref, out_hbm, stage, sems):
    rows, lags = stage.shape
    turned = summed_ref[...].T
    high = turned.astype(BF16)
    low = (turned - high.astype(F32)).astype(BF16)
    both = jnp.concatenate([high, low], axis=0)
    step = lags // 2
    copies = []
    for j in range(2):
        at = slice(j * step, (j + 1) * step)
        out = jnp.dot(both, high_ref[:, at], preferred_element_type=F32)
        stage[:, at] = out[:rows] + out[rows:] + jnp.dot(high, low_ref[:, at], preferred_element_type=F32)
        copies.append(pltpu.make_async_copy(stage.at[:, at], out_hbm.at[:, at], sems.at[j]))
        copies[j].start()
    for copy in copies:
        copy.wait()


def call(kernel, out_shape, in_specs, out_specs, scratch=()):
    return pl.pallas_call(
        kernel,
        out_shape=out_shape,
        in_specs=in_specs,
        out_specs=out_specs,
        scratch_shapes=list(scratch),
        compiler_params=pltpu.CompilerParams(vmem_limit_bytes=48 * 1024 * 1024),
    )


def local(spectra, picks, pair_own, pair_far, pair_mask):
    n_sta = lax.axis_size("sta")
    n_day = lax.axis_size("day")
    _, stations, width = spectra.shape
    bins = width // 2
    part = bins // n_day
    pairs = pair_own.shape[0]
    mine_pairs = pairs // n_day
    slots = n_sta * SLOTS
    shape = jax.ShapeDtypeStruct
    dma = pltpu.SemaphoreType.DMA
    own, far, mask = [a.reshape(n_day, mine_pairs) for a in (pair_own, pair_far, pair_mask)]

    by_bin = call(turn_kernel, shape((n_day, part, 2 * stations), BF16), [VMEM], VMEM)(spectra)
    mine = lax.all_to_all(by_bin, "day", split_axis=0, concat_axis=0, tiled=True)
    chosen = call(pick_kernel, shape((n_sta, SLOTS, width), BF16), [VMEM] * 2, VMEM)(picks[0].T, mine)
    got = lax.all_to_all(chosen, "sta", split_axis=0, concat_axis=0, tiled=True).reshape(slots, width)
    cross = call(
        cross_kernel,
        shape((n_day, 2 * part, mine_pairs), F32),
        [VMEM] * 5,
        VMEM,
        [pltpu.VMEM((width, slots), BF16)],
    )(own, far, mask, mine, got)
    summed = lax.all_to_all(cross, "day", split_axis=0, concat_axis=0, tiled=True).reshape(width, mine_pairs)
    high, low = lag_table(bins, n_day, 1.0 / np.sqrt(width * n_day))
    return call(
        stack_kernel,
        shape((mine_pairs, LAGS), F32),
        [VMEM] * 3,
        HBM,
        [pltpu.VMEM((mine_pairs, LAGS), F32), dma((2,))],
    )(summed, jnp.asarray(high), jnp.asarray(low))


def solution(mesh):
    in_specs = (P("day", "sta", None), P("sta", None, None), P("sta"), P("sta"), P("sta"))
    out_specs = P(("sta", "day"), None)
    return jax.shard_map(local, mesh=mesh, in_specs=in_specs, out_specs=out_specs, check_vma=False)
```

```python
import jax
import jax.numpy as jnp
import numpy as np
from jax import lax
from jax.experimental import pallas as pl
from jax.experimental.pallas import tpu as pltpu
from jax.sharding import PartitionSpec as P

SLOTS = 8
LAGS = 1024
BASE = 40
BF16 = jnp.bfloat16
F32 = jnp.float32
VMEM = pl.BlockSpec(memory_space=pltpu.VMEM)
HBM = pl.BlockSpec(memory_space=pltpu.HBM)


def lag_table(bins, n_day, scale):
    k = np.concatenate([np.arange(0, bins, 2), np.arange(1, bins, 2)])[:, None] + BASE
    m = np.arange(LAGS // 2)[None, :] - LAGS // 2
    angle = 2.0 * np.pi / LAGS * (k * m % LAGS)
    part = bins // n_day
    both = np.stack([np.cos(angle), -np.sin(angle)]) * scale
    both = both.reshape(2, n_day, part, -1).transpose(1, 0, 2, 3).reshape(2 * bins, -1).astype(np.float32)
    high = both.astype(jnp.bfloat16)
    low = (both - high.astype(np.float32)).astype(jnp.bfloat16)
    return high, low


def open_kernel(x_hbm, picks_hbm, own_hbm, mask_hbm, far_hbm, by_bin_ref, picks_ref, row_ref, far_ref, *scratch):
    x_ref, own_ref, mask_ref, turned, sems = scratch
    copies = [
        pltpu.make_async_copy(source, target, sems.at[i])
        for i, (source, target) in enumerate(
            [(x_hbm, x_ref), (picks_hbm, picks_ref), (own_hbm, own_ref), (mask_hbm, mask_ref), (far_hbm, far_ref)]
        )
    ]
    for copy in copies:
        copy.start()
    bins, twice = turned.shape
    for copy in copies[1:]:
        copy.wait()
    row_ref[...] = jnp.where(mask_ref[...] > 0, own_ref[...], 2 * twice)
    copies[0].wait()
    x = x_ref[0].astype(F32)
    turned[...] = jnp.concatenate([x[:, :bins], x[:, bins:]], axis=0).T
    by_parity = [turned[pl.ds(odd, bins // 2, stride=2), :] for odd in range(2)]
    by_bin_ref[...] = jnp.concatenate(by_parity, axis=0).astype(BF16).reshape(by_bin_ref.shape)


def pick_kernel(picks_ref, mine_ref, out_ref):
    slots, owners = picks_ref.shape
    n_day, part, twice = mine_ref.shape
    stations = twice // 2
    turned = mine_ref[...].reshape(n_day * part, twice).T
    source = jnp.concatenate([turned[:stations], turned[stations:]], axis=1)
    picks = picks_ref[...]
    lane = lax.broadcasted_iota(jnp.int32, (slots, stations), 1)
    hot = jnp.concatenate([(lane == picks[:, o : o + 1]).astype(F32) for o in range(owners)], axis=0).astype(BF16)
    got = jnp.dot(hot, source, preferred_element_type=F32)
    out_ref[...] = got.astype(BF16).reshape(out_ref.shape)


def cross_kernel(own_ref, far_ref, mine_ref, got_ref, out_ref, turned):
    n_day, part, twice = mine_ref.shape
    rows = n_day * part
    blocks, lanes = own_ref.shape
    mine = mine_ref[...].reshape(rows, twice)
    turned[...] = got_ref[...].T
    near_row = lax.broadcasted_iota(jnp.int32, (twice, 2 * lanes), 0)
    far_row = lax.broadcasted_iota(jnp.int32, (got_ref.shape[0], 2 * lanes), 0)
    for j in range(0, blocks, 2):
        own = jnp.concatenate([own_ref[j : j + 1, :], own_ref[j + 1 : j + 2, :]], axis=1)
        far = jnp.concatenate([far_ref[j : j + 1, :], far_ref[j + 1 : j + 2, :]], axis=1)
        hot_far = (far_row == far).astype(F32).astype(BF16)
        both = jnp.dot(turned[...], hot_far, preferred_element_type=F32)
        hot_re = (near_row == own).astype(F32).astype(BF16)
        hot_im = (near_row == own + twice // 2).astype(F32).astype(BF16)
        near_re = jnp.dot(mine, hot_re, preferred_element_type=F32)
        near_im = jnp.dot(mine, hot_im, preferred_element_type=F32)
        far_re, far_im = both[:rows], both[rows:]
        real = jnp.sum((near_re * far_re + near_im * far_im).reshape(n_day, part, 2 * lanes), axis=0)
        imag = jnp.sum((near_im * far_re - near_re * far_im).reshape(n_day, part, 2 * lanes), axis=0)
        for i in range(2):
            out_ref[j + i, :part, :] = real[:, i * lanes : (i + 1) * lanes]
            out_ref[j + i, part:, :] = imag[:, i * lanes : (i + 1) * lanes]


def stack_kernel(summed_ref, high_ref, low_ref, out_hbm, stage, sems):
    rows, lags = stage.shape
    turned = summed_ref[...].T
    high = turned.astype(BF16)
    low = (turned - high.astype(F32)).astype(BF16)
    both = jnp.concatenate([high, low], axis=0)
    depth = both.shape[1] // 2
    step = lags // 4
    copies = []
    for j in range(2):
        at = slice(j * step, (j + 1) * step)
        sums = []
        for odd in range(2):
            bins = slice(odd * depth, (odd + 1) * depth)
            out = jnp.dot(both[:, bins], high_ref[bins, at], preferred_element_type=F32)
            out_low = jnp.dot(high[:, bins], low_ref[bins, at], preferred_element_type=F32)
            sums.append(out[:rows] + out[rows:] + out_low)
        for half, total in enumerate((sums[0] + sums[1], sums[0] - sums[1])):
            to = slice(half * lags // 2 + j * step, half * lags // 2 + (j + 1) * step)
            stage[:, to] = total
            copies.append(pltpu.make_async_copy(stage.at[:, to], out_hbm.at[:, to], sems.at[2 * j + half]))
            copies[-1].start()
    for copy in copies:
        copy.wait()


def call(kernel, out_shape, in_specs, out_specs, scratch=()):
    return pl.pallas_call(
        kernel,
        out_shape=out_shape,
        in_specs=in_specs,
        out_specs=out_specs,
        scratch_shapes=list(scratch),
        compiler_params=pltpu.CompilerParams(vmem_limit_bytes=48 * 1024 * 1024),
    )


def local(spectra, picks, pair_own, pair_far, pair_mask):
    n_sta = lax.axis_size("sta")
    n_day = lax.axis_size("day")
    _, stations, width = spectra.shape
    bins = width // 2
    part = bins // n_day
    pairs = pair_own.shape[0]
    mine_pairs = pairs // n_day
    slots = n_sta * SLOTS
    shape = jax.ShapeDtypeStruct
    dma = pltpu.SemaphoreType.DMA
    own, far, mask = [a.reshape(n_day, mine_pairs) for a in (pair_own, pair_far, pair_mask)]

    given = [pltpu.with_memory_space_constraint(a, pltpu.HBM) for a in (spectra, picks[0].T, own, mask, far)]
    by_bin, picks, rows, far = call(
        open_kernel,
        (
            shape((n_day, part, 2 * stations), BF16),
            shape((SLOTS, n_sta), jnp.int32),
            shape((n_day, mine_pairs), jnp.int32),
            shape((n_day, mine_pairs), jnp.int32),
        ),
        [HBM] * 5,
        (VMEM,) * 4,
        [pltpu.VMEM(a.shape, a.dtype) for a in (spectra, own, mask)] + [pltpu.VMEM((bins, 2 * stations), F32), dma((5,))],
    )(*given)
    mine = lax.all_to_all(by_bin, "day", split_axis=0, concat_axis=0, tiled=True)
    chosen = call(pick_kernel, shape((n_sta, SLOTS, width), BF16), [VMEM] * 2, VMEM)(picks, mine)
    got = lax.all_to_all(chosen, "sta", split_axis=0, concat_axis=0, tiled=True).reshape(slots, width)
    cross = call(
        cross_kernel,
        shape((n_day, 2 * part, mine_pairs), F32),
        [VMEM] * 4,
        VMEM,
        [pltpu.VMEM((width, slots), BF16)],
    )(rows, far, mine, got)
    summed = lax.all_to_all(cross, "day", split_axis=0, concat_axis=0, tiled=True).reshape(width, mine_pairs)
    high, low = lag_table(bins, n_day, 1.0 / np.sqrt(width * n_day))
    return call(
        stack_kernel,
        shape((mine_pairs, LAGS), F32),
        [VMEM] * 3,
        HBM,
        [pltpu.VMEM((mine_pairs, LAGS), F32), dma((4,))],
    )(summed, jnp.asarray(high), jnp.asarray(low))


def solution(mesh):
    in_specs = (P("day", "sta", None), P("sta", None, None), P("sta"), P("sta"), P("sta"))
    out_specs = P(("sta", "day"), None)
    return jax.shard_map(local, mesh=mesh, in_specs=in_specs, out_specs=out_specs, check_vma=False)
```

```python
import jax
import jax.numpy as jnp
import numpy as np
from jax import lax
from jax.experimental import pallas as pl
from jax.experimental.pallas import tpu as pltpu
from jax.sharding import PartitionSpec as P

SLOTS = 8
LAGS = 1024
BASE = 40
PIECES = 2
BF16 = jnp.bfloat16
F32 = jnp.float32
VMEM = pl.BlockSpec(memory_space=pltpu.VMEM)
HBM = pl.BlockSpec(memory_space=pltpu.HBM)


def lag_table(bins, n_day, scale):
    k = np.concatenate([np.arange(0, bins, 2), np.arange(1, bins, 2)])[:, None] + BASE
    m = np.arange(LAGS // 2)[None, :] - LAGS // 2
    angle = 2.0 * np.pi / LAGS * (k * m % LAGS)
    part = bins // n_day
    both = np.stack([np.cos(angle), -np.sin(angle)]) * scale
    both = both.reshape(2, n_day, part, -1).transpose(1, 0, 2, 3).reshape(2 * bins, -1).astype(np.float32)
    high = both.astype(jnp.bfloat16)
    low = (both - high.astype(np.float32)).astype(jnp.bfloat16)
    return high, low


def open_kernel(x_hbm, picks_hbm, own_hbm, mask_hbm, far_hbm, by_bin_ref, picks_ref, row_ref, far_ref, *scratch):
    x_ref, own_ref, mask_ref, turned, sems = scratch
    step = x_ref.shape[1] // PIECES
    pieces = [pl.ds(i * step, step) for i in range(PIECES)]
    copies = [
        pltpu.make_async_copy(source, target, sems.at[i])
        for i, (source, target) in enumerate(
            [(x_hbm.at[:, at], x_ref.at[:, at]) for at in pieces]
            + [(picks_hbm, picks_ref), (own_hbm, own_ref), (mask_hbm, mask_ref), (far_hbm, far_ref)]
        )
    ]
    for copy in copies:
        copy.start()
    bins, twice = turned.shape
    for copy in copies[PIECES:]:
        copy.wait()
    row_ref[...] = jnp.where(mask_ref[...] > 0, own_ref[...], 2 * twice)
    for copy in copies[:PIECES]:
        copy.wait()
    x = x_ref[0].astype(F32)
    turned[...] = jnp.concatenate([x[:, :bins], x[:, bins:]], axis=0).T
    by_parity = [turned[pl.ds(odd, bins // 2, stride=2), :] for odd in range(2)]
    by_bin_ref[...] = jnp.concatenate(by_parity, axis=0).astype(BF16).reshape(by_bin_ref.shape)


def pick_kernel(picks_ref, mine_ref, out_ref):
    slots, owners = picks_ref.shape
    n_day, part, twice = mine_ref.shape
    stations = twice // 2
    turned = mine_ref[...].reshape(n_day * part, twice).T
    source = jnp.concatenate([turned[:stations], turned[stations:]], axis=1)
    picks = picks_ref[...]
    lane = lax.broadcasted_iota(jnp.int32, (slots, stations), 1)
    hot = jnp.concatenate([(lane == picks[:, o : o + 1]).astype(F32) for o in range(owners)], axis=0).astype(BF16)
    got = jnp.dot(hot, source, preferred_element_type=F32)
    out_ref[...] = got.astype(BF16).reshape(out_ref.shape)


def cross_kernel(own_ref, far_ref, mine_ref, got_ref, out_ref, turned):
    n_day, part, twice = mine_ref.shape
    rows = n_day * part
    blocks, lanes = own_ref.shape
    mine = mine_ref[...].reshape(rows, twice)
    turned[...] = got_ref[...].T
    near_row = lax.broadcasted_iota(jnp.int32, (twice, 2 * lanes), 0)
    far_row = lax.broadcasted_iota(jnp.int32, (got_ref.shape[0], 2 * lanes), 0)
    for j in range(0, blocks, 2):
        own = jnp.concatenate([own_ref[j : j + 1, :], own_ref[j + 1 : j + 2, :]], axis=1)
        far = jnp.concatenate([far_ref[j : j + 1, :], far_ref[j + 1 : j + 2, :]], axis=1)
        hot_far = (far_row == far).astype(F32).astype(BF16)
        both = jnp.dot(turned[...], hot_far, preferred_element_type=F32)
        hot_re = (near_row == own).astype(F32).astype(BF16)
        hot_im = (near_row == own + twice // 2).astype(F32).astype(BF16)
        near_re = jnp.dot(mine, hot_re, preferred_element_type=F32)
        near_im = jnp.dot(mine, hot_im, preferred_element_type=F32)
        far_re, far_im = both[:rows], both[rows:]
        real = jnp.sum((near_re * far_re + near_im * far_im).reshape(n_day, part, 2 * lanes), axis=0)
        imag = jnp.sum((near_im * far_re - near_re * far_im).reshape(n_day, part, 2 * lanes), axis=0)
        for i in range(2):
            out_ref[j + i, :part, :] = real[:, i * lanes : (i + 1) * lanes]
            out_ref[j + i, part:, :] = imag[:, i * lanes : (i + 1) * lanes]


def stack_kernel(summed_ref, high_ref, low_ref, out_hbm, stage, sems):
    rows, lags = stage.shape
    turned = summed_ref[...].T
    high = turned.astype(BF16)
    low = (turned - high.astype(F32)).astype(BF16)
    both = jnp.concatenate([high, low], axis=0)
    depth = both.shape[1] // 2
    step = lags // 4
    copies = []
    for j in range(2):
        at = slice(j * step, (j + 1) * step)
        sums = []
        for odd in range(2):
            bins = slice(odd * depth, (odd + 1) * depth)
            out = jnp.dot(both[:, bins], high_ref[bins, at], preferred_element_type=F32)
            out_low = jnp.dot(high[:, bins], low_ref[bins, at], preferred_element_type=F32)
            sums.append(out[:rows] + out[rows:] + out_low)
        for half, total in enumerate((sums[0] + sums[1], sums[0] - sums[1])):
            to = slice(half * lags // 2 + j * step, half * lags // 2 + (j + 1) * step)
            stage[:, to] = total
            copies.append(pltpu.make_async_copy(stage.at[:, to], out_hbm.at[:, to], sems.at[2 * j + half]))
            copies[-1].start()
    for copy in copies:
        copy.wait()


def call(kernel, out_shape, in_specs, out_specs, scratch=()):
    return pl.pallas_call(
        kernel,
        out_shape=out_shape,
        in_specs=in_specs,
        out_specs=out_specs,
        scratch_shapes=list(scratch),
        compiler_params=pltpu.CompilerParams(vmem_limit_bytes=48 * 1024 * 1024),
    )


def local(spectra, picks, pair_own, pair_far, pair_mask):
    n_sta = lax.axis_size("sta")
    n_day = lax.axis_size("day")
    _, stations, width = spectra.shape
    bins = width // 2
    part = bins // n_day
    pairs = pair_own.shape[0]
    mine_pairs = pairs // n_day
    slots = n_sta * SLOTS
    shape = jax.ShapeDtypeStruct
    dma = pltpu.SemaphoreType.DMA
    own, far, mask = [a.reshape(n_day, mine_pairs) for a in (pair_own, pair_far, pair_mask)]

    given = [pltpu.with_memory_space_constraint(a, pltpu.HBM) for a in (spectra, picks[0].T, own, mask, far)]
    by_bin, picks, rows, far = call(
        open_kernel,
        (
            shape((n_day, part, 2 * stations), BF16),
            shape((SLOTS, n_sta), jnp.int32),
            shape((n_day, mine_pairs), jnp.int32),
            shape((n_day, mine_pairs), jnp.int32),
        ),
        [HBM] * 5,
        (VMEM,) * 4,
        [pltpu.VMEM(a.shape, a.dtype) for a in (spectra, own, mask)] + [pltpu.VMEM((bins, 2 * stations), F32), dma((4 + PIECES,))],
    )(*given)
    mine = lax.all_to_all(by_bin, "day", split_axis=0, concat_axis=0, tiled=True)
    chosen = call(pick_kernel, shape((n_sta, SLOTS, width), BF16), [VMEM] * 2, VMEM)(picks, mine)
    got = lax.all_to_all(chosen, "sta", split_axis=0, concat_axis=0, tiled=True).reshape(slots, width)
    cross = call(
        cross_kernel,
        shape((n_day, 2 * part, mine_pairs), F32),
        [VMEM] * 4,
        VMEM,
        [pltpu.VMEM((width, slots), BF16)],
    )(rows, far, mine, got)
    summed = lax.all_to_all(cross, "day", split_axis=0, concat_axis=0, tiled=True).reshape(width, mine_pairs)
    high, low = lag_table(bins, n_day, 1.0 / np.sqrt(width * n_day))
    return call(
        stack_kernel,
        shape((mine_pairs, LAGS), F32),
        [VMEM] * 3,
        HBM,
        [pltpu.VMEM((mine_pairs, LAGS), F32), dma((4,))],
    )(summed, jnp.asarray(high), jnp.asarray(low))


def solution(mesh):
    in_specs = (P("day", "sta", None), P("sta", None, None), P("sta"), P("sta"), P("sta"))
    out_specs = P(("sta", "day"), None)
    return jax.shard_map(local, mesh=mesh, in_specs=in_specs, out_specs=out_specs, check_vma=False)
```
